128 devices in a mesh: dp: 4 (over y), expert: 32 (over x, z, core).
Axes of the slice: x: 4, y: 4, z: 4, core: 2. Of those that a mesh axis runs over, the one named last changes fastest.
Arguments:
- tokens: bfloat16 [16384, 2560], P(('dp', 'expert')), may hold values from -6 to 6
- cotangent: bfloat16 [16384, 2560], P(('dp', 'expert')), may hold values from -4 to 4
- expert_ids: int32 [16384, 6], P(('dp', 'expert')), may hold values from 0 to 31, all different within a row; in each aligned block of 128 rows (0 to 127, 128 to 255, ...) at most 48 rows name the same one
- router_probs: float32 [16384, 6], P(('dp', 'expert')), may hold values from 0.05 to 1
- spare_replica: int32 [32, 4], P('expert'), may hold values from 0 to 3, as said below
- w_gate: bfloat16 [32, 2560, 832], P('expert'), may hold values from -0.125 to 0.125
- w_up: bfloat16 [32, 2560, 832], P('expert'), may hold values from -0.125 to 0.125
- w_down: bfloat16 [32, 832, 2560], P('expert'), may hold values from -0.21875 to 0.21875
Outputs:
- token_grad: bfloat16 [16384, 2560], P(('dp', 'expert'))
- prob_grad: float32 [16384, 6], P(('dp', 'expert'))
- grad_gate: bfloat16 [32, 2560, 832], P('expert', 'dp')
- grad_up: bfloat16 [32, 2560, 832], P('expert', 'dp')
- grad_down: bfloat16 [32, 832, 2560], P('expert', 'dp')
The draws below stay inside these ranges and needn't reach their ends.
Inputs may be any that keep to these rules, and one draw needn't show every extreme that they name: `expert_ids`: each token names 6 different experts. Among the 128 tokens of one device no expert is named by more than 48 tokens, and in every draw some device has an expert named by exactly 48 of its tokens. spare_replica[e, r] == r means that dp row r has no spare replica for expert e.
All inputs are finite; a program needn't handle non-finite values.
Results may differ from the reference program's by a relative error of at most 0.014.
Values may be sent and summed in bfloat16 or wider, within the bound.
No kernel may reach another device: no remote copies, remote signals or barrier semaphores. Data moves between devices by JAX's collectives and lax.ppermute only.
A program may use at most 192 MiB of HBM per device.

```python
import math
import jax
import jax.numpy as jnp
import numpy as np
from jax import lax

D = 2560
TOP = 6
FF = 832
TOK_DEV = 128
EXPERTS = 32
REPLICAS = 4
TOKENS = 16384
MOST = 48
CAP = 768
SPARE = 96
SLOTS = 864


def draw_spare_replica(key, part):
    key = jax.random.fold_in(key, 11)
    picked = jax.random.randint(key, (EXPERTS, REPLICAS), 0, REPLICAS)
    return picked.astype(jnp.int32)


def steps_of(stream_key, dims, pieces, low, largest):
    gain, own = 1.0, jax.random.fold_in(stream_key, 6)
    for axis_at, parts in pieces:
        heights = jnp.exp(jax.random.uniform(jax.random.fold_in(own, axis_at), (parts,), jnp.float32, low / len(pieces), largest / len(pieces)))
        gain = gain * jnp.repeat(heights, dims[axis_at] // parts).reshape([-1 if axis == axis_at else 1 for axis in range(len(dims))])
    return gain


def deal_out(key, own, number, rows, amount, top, limit, slope):
    ranking = jax.random.permutation(key, amount)
    heavy_load, common = portions_of(amount, rows * top, limit, slope, True), portions_of(amount, rows * top, limit, slope, False)
    places = jnp.arange(amount)

    def named(tallies, rotation):
        used = int((tallies > 0).sum())
        fixed = max(1, used // 4)
        shifted = fixed + (places - fixed + rotation * (used - fixed)) % max(1, amount - fixed)
        return jnp.zeros((amount,), jnp.int32).at[ranking[jnp.where(places < fixed, places, shifted)]].set(jnp.asarray(tallies, jnp.int32))

    tallies = jnp.where(number % 4 == 0, named(heavy_load, number // 4), named(common, number - number // 4 - 1))
    mixed = jax.random.permutation(jax.random.fold_in(own, 3), amount)
    donor, taker = mixed[0:amount // 2 * 2:2], mixed[1:amount // 2 * 2:2]
    margin = jnp.minimum(tallies[donor] - 1, limit - tallies[taker]) // 2
    margin = jnp.where((donor == ranking[0]) | (taker == ranking[0]) | (tallies[taker] == 0), 0, jnp.maximum(margin, 0))
    shifted = jax.random.randint(jax.random.fold_in(own, 4), (amount // 2,), 0, 1 << 20) % (margin + 1)
    tallies = tallies.at[donor].add(-shifted).at[taker].add(shifted)
    members = jnp.searchsorted(jnp.cumsum(tallies), jnp.arange(rows * top), side="right").astype(jnp.int32)
    grid = members.reshape(top, rows).T
    grid = grid[jax.random.permutation(jax.random.fold_in(own, 1), rows)]
    rotation = jax.random.randint(jax.random.fold_in(own, 2), (rows, 1), 0, top)
    return jnp.take_along_axis(grid, (jnp.arange(top)[None, :] + rotation) % top, axis=1)


def portions_of(amount, total, most, skew, full):
    weights = [(1 << 20) // math.isqrt(standing ** skew) + 1 for standing in range(1, amount + 1)]
    largest = most if full else min(most, max(-(-total // amount), total * weights[0] // sum(weights)))
    least = 1 if total - largest >= amount - 1 else 0
    given, surplus = [largest] + [least] * (amount - 1), total - largest - least * (amount - 1)
    while surplus > 0:
        candidates = [i for i in range(1, amount) if given[i] < largest] or [i for i in range(1, amount) if given[i] < most]
        whole, remaining = sum([weights[i] for i in candidates]), surplus
        for i in candidates:
            addition = min(most - given[i], max(1, remaining * weights[i] // whole), surplus)
            given[i] = given[i] + addition
            surplus = surplus - addition
    return np.array(given)


def normal_values(rng, dims, deviation, reach, cuts=(), held_as=jnp.bfloat16):
    drawn = jax.random.normal(rng, dims, jnp.float32) * deviation
    if len(cuts) > 0:
        drawn = steps_of(rng, dims, cuts, -0.22, 0.18) * drawn
    return jnp.clip(drawn, min=-reach, max=reach).astype(held_as)


def setup_inputs(seed: int = 0) -> dict:
    key_of = jax.random.split(jax.random.key(seed), 9)
    tokens = normal_values(key_of[0], (TOKENS, D), 1.0, 6.0, ((0, 128),))
    cotangent = normal_values(key_of[1], (TOKENS, D), 0.5, 4.0, ((0, 128),))
    expert_ids_keys = jax.random.split(jax.random.fold_in(key_of[2], 1), TOKENS // TOK_DEV)
    expert_ids_turns = jax.random.permutation(jax.random.fold_in(key_of[2], 3), TOKENS // TOK_DEV)
    expert_ids = jax.vmap(lambda own, number: deal_out(jax.random.fold_in(key_of[2], 2), own, number, TOK_DEV, EXPERTS, TOP, MOST, 2))(expert_ids_keys, expert_ids_turns).reshape((TOKENS, TOP))
    router_probs = jnp.clip(jnp.exp(math.log(1.0) - 2.9957323 * jax.random.uniform(key_of[3], (TOKENS, TOP), jnp.float32) ** steps_of(key_of[3], (TOKENS, TOP), ((0, 128),), -0.2, 0.2)), 0.05, 1.0)
    spare_replica = draw_spare_replica(jax.random.fold_in(key_of[8], 71), 0)
    w_gate = normal_values(key_of[5], (EXPERTS, D, FF), D ** -0.5, 0.125, ((0, 32),))
    w_up = normal_values(key_of[6], (EXPERTS, D, FF), D ** -0.5, 0.125, ((0, 32),))
    w_down = normal_values(key_of[7], (EXPERTS, FF, D), FF ** -0.5, 0.21875, ((0, 32),))
    return dict(tokens=tokens, cotangent=cotangent, expert_ids=expert_ids, router_probs=router_probs, spare_replica=spare_replica, w_gate=w_gate, w_up=w_up, w_down=w_down)


def replica_work(rows_in, cot_rows, scales, gate, upper, lower):
    hidden = jnp.dot(rows_in, gate, preferred_element_type=jnp.float32)
    lifted = jnp.dot(rows_in, upper, preferred_element_type=jnp.float32)
    logistic = jax.nn.sigmoid(hidden)
    swished = hidden * logistic
    activated = (swished * lifted).astype(jnp.bfloat16)
    pulled = lax.dot_general(cot_rows, lower, (((1,), (1,)), ((), ())), preferred_element_type=jnp.float32)
    shares = jnp.sum(activated.astype(jnp.float32) * pulled, axis=1).astype(jnp.bfloat16)
    grad_act = scales.astype(jnp.float32)[:, None] * pulled
    grad_hidden = (grad_act * lifted * logistic * (1.0 + hidden * (1.0 - logistic))).astype(jnp.bfloat16)
    grad_lifted = (grad_act * swished).astype(jnp.bfloat16)
    back_rows = lax.dot_general(grad_hidden, gate, (((1,), (1,)), ((), ())), preferred_element_type=jnp.float32)
    back_rows = back_rows + lax.dot_general(grad_lifted, upper, (((1,), (1,)), ((), ())), preferred_element_type=jnp.float32)
    back_rows = back_rows.astype(jnp.bfloat16)
    grad_out = (scales.astype(jnp.float32)[:, None] * cot_rows.astype(jnp.float32)).astype(jnp.bfloat16)
    part_gate = lax.dot_general(rows_in, grad_hidden, (((0,), (0,)), ((), ())), preferred_element_type=jnp.float32)
    part_upper = lax.dot_general(rows_in, grad_lifted, (((0,), (0,)), ((), ())), preferred_element_type=jnp.float32)
    part_lower = lax.dot_general(activated, grad_out, (((0,), (0,)), ((), ())), preferred_element_type=jnp.float32)
    return back_rows, shares, part_gate, part_upper, part_lower


def reference(tokens, cotangent, expert_ids, router_probs, spare_replica, w_gate, w_up, w_down):
    rows_all = TOKENS * TOP
    per_row = rows_all // REPLICAS
    total = jnp.sum(router_probs, axis=1, keepdims=True)
    scale = router_probs / total
    scale_b = scale.astype(jnp.bfloat16)
    flat_ids = expert_ids.reshape(REPLICAS, per_row).astype(jnp.int32)
    expert_iota = jnp.arange(EXPERTS).astype(jnp.int32)
    onehot = (flat_ids[:, :, None] == expert_iota[None, None, :]).astype(jnp.int32)
    running = jnp.cumsum(onehot, axis=1)
    position = (jnp.sum(running * onehot, axis=2) - 1).astype(jnp.int32)
    load = running[:, -1, :]
    excess = jnp.maximum(load - CAP, 0)
    spare_of = spare_replica.T.astype(jnp.int32)
    replica_iota = jnp.arange(REPLICAS).astype(jnp.int32)
    sends = spare_of != replica_iota[:, None]
    same = spare_of[:, None, :] == spare_of[None, :, :]
    earlier = replica_iota[None, :] < replica_iota[:, None]
    offset = jnp.sum(jnp.where(same & earlier[:, :, None] & sends[None, :, :], excess[None, :, :], 0), axis=1).astype(jnp.int32)
    offset_row = jnp.take_along_axis(offset, flat_ids, axis=1)
    spare_row = jnp.take_along_axis(spare_of, flat_ids, axis=1)
    spare_slot = offset_row + position - CAP
    at_home = position < CAP
    home_dp = jnp.broadcast_to(replica_iota[:, None], (REPLICAS, per_row))
    at_spare = jnp.logical_not(at_home) & (spare_slot < SPARE) & (spare_row != home_dp)
    replica = jnp.where(at_home, home_dp, spare_row)
    slot = jnp.where(at_home, position, CAP + spare_slot)
    slot_count = REPLICAS * EXPERTS * SLOTS
    target = jnp.where(at_home | at_spare, (replica * EXPERTS + flat_ids) * SLOTS + slot, slot_count).astype(jnp.int32)
    row_index = jnp.arange(rows_all).astype(jnp.int32)
    table = jnp.full((slot_count,), rows_all, jnp.int32).at[target.reshape(-1)].set(row_index, mode="drop")
    table = table.reshape(REPLICAS, EXPERTS, SLOTS).transpose(1, 0, 2).reshape(EXPERTS, REPLICAS * SLOTS)
    tokens_ext = jnp.concatenate([tokens, jnp.zeros((1, D), tokens.dtype)], axis=0)
    cot_ext = jnp.concatenate([cotangent, jnp.zeros((1, D), cotangent.dtype)], axis=0)
    scale_ext = jnp.concatenate([scale_b.reshape(-1), jnp.zeros((1,), scale_b.dtype)], axis=0)

    def one_expert(carry, inputs):
        token_acc, share_acc = carry
        row_ids, gate, upper, lower = inputs
        tok_ids = (row_ids // TOP).astype(jnp.int32)
        rows_in = tokens_ext[tok_ids]
        cot_rows = cot_ext[tok_ids]
        scales = scale_ext[row_ids]
        backs = []
        shares = []
        sum_gate = jnp.zeros((D, FF), jnp.float32)
        sum_upper = jnp.zeros((D, FF), jnp.float32)
        sum_lower = jnp.zeros((FF, D), jnp.float32)
        for replica_no in range(REPLICAS):
            low = replica_no * SLOTS
            result = replica_work(rows_in[low:low + SLOTS], cot_rows[low:low + SLOTS], scales[low:low + SLOTS], gate, upper, lower)
            backs.append(result[0])
            shares.append(result[1])
            sum_gate = sum_gate + result[2].astype(jnp.bfloat16).astype(jnp.float32)
            sum_upper = sum_upper + result[3].astype(jnp.bfloat16).astype(jnp.float32)
            sum_lower = sum_lower + result[4].astype(jnp.bfloat16).astype(jnp.float32)
        back_rows = jnp.concatenate(backs, axis=0)
        share_rows = jnp.concatenate(shares, axis=0)
        token_acc = token_acc.at[tok_ids].add(back_rows.astype(jnp.float32), mode="drop")
        share_acc = share_acc.at[row_ids].set(share_rows.astype(jnp.float32), mode="drop")
        outputs = (sum_gate.astype(jnp.bfloat16), sum_upper.astype(jnp.bfloat16), sum_lower.astype(jnp.bfloat16))
        return (token_acc, share_acc), outputs

    start = (jnp.zeros((TOKENS, D), jnp.float32), jnp.zeros((rows_all,), jnp.float32))
    (token_acc, share_acc), grads = lax.scan(one_expert, start, (table, w_gate, w_up, w_down))
    token_grad = token_acc.astype(jnp.bfloat16)
    share = share_acc.reshape(TOKENS, TOP)
    prob_grad = (share - jnp.sum(scale * share, axis=1, keepdims=True)) / total
    return token_grad, prob_grad, grads[0], grads[1], grads[2]
```

```python
import jax
import jax.numpy as jnp
from jax import lax
from jax.sharding import PartitionSpec as P

BF = jnp.bfloat16
F32 = jnp.float32
SIDE = 4
N_REP = 4
N_EXP = 32


def chip_perm(step):
    out = []
    for x in range(SIDE):
        for z in range(SIDE):
            for core in range(2):
                x2, z2, core2 = step(x, z, core)
                out.append(((x * SIDE + z) * 2 + core, (x2 * SIDE + z2) * 2 + core2))
    return out


def along_x(v, by):
    return lax.ppermute(v, "expert", chip_perm(lambda x, z, c: ((x + by) % SIDE, z, c)))


def along_z(v, by):
    return lax.ppermute(v, "expert", chip_perm(lambda x, z, c: (x, (z + by) % SIDE, c)))


def along_y(v, by):
    return lax.ppermute(v, "dp", [(r, (r + by) % N_REP) for r in range(N_REP)])


def other_core(v):
    return lax.ppermute(v, "expert", chip_perm(lambda x, z, c: (x, z, 1 - c)))


def ring_reduce(part, shift):
    far = part(2).astype(BF)
    half = far.shape[0] // 2
    low = shift(far[:half], 1)
    high = shift(far[half:], -1)
    near = part(1)
    ahead = jnp.concatenate([near[:half] + low.astype(F32), near[half:]], axis=0).astype(BF)
    got_a = shift(ahead, 1)
    near = part(3)
    behind = jnp.concatenate([near[:half], near[half:] + high.astype(F32)], axis=0).astype(BF)
    got_b = shift(behind, -1)
    return part(0) + got_a.astype(F32) + got_b.astype(F32)


def one_hot(slot, slots):
    return (lax.broadcasted_iota(jnp.int32, (slots, slot.shape[0]), 0) == slot[None, :]).astype(BF)


def placement(ids, scale, spares, expert, rep, cap, spare_cap):
    named = jnp.any(ids == expert, axis=2).astype(F32)
    load = jnp.sum(named, axis=(1, 2)).astype(jnp.int32)
    excess = jnp.maximum(load - cap, 0)
    iota = jnp.arange(N_REP, dtype=jnp.int32)
    same = spares == spares[rep]
    offset = jnp.sum(jnp.where(same & (iota < rep) & (spares != iota), excess, 0))
    extra = jnp.where(spares[rep] != rep, jnp.maximum(spare_cap - offset, 0), 0)
    limit = cap + extra
    mine = lax.dynamic_index_in_dim(named, rep, 0, keepdims=False)
    blocks, count = mine.shape
    upto = (
        lax.broadcasted_iota(jnp.int32, (count, count), 0)
        <= lax.broadcasted_iota(jnp.int32, (count, count), 1)
    ).astype(BF)
    running = jnp.dot(mine.astype(BF), upto, preferred_element_type=F32).astype(jnp.int32)
    totals = running[:, -1]
    before = jnp.cumsum(totals) - totals
    position = before[:, None] + running - 1
    placed = (mine > 0) & (position < limit)
    ids_here = lax.dynamic_index_in_dim(ids, rep, 0, keepdims=False)
    weight = jnp.sum(jnp.where(ids_here == expert, scale.astype(F32), 0.0), axis=1)
    return jnp.where(placed, position, -1), weight


def local(tokens, cotangent, expert_ids, router_probs, spare_replica, w_gate, w_up, w_down):
    rep = lax.axis_index("dp")
    expert = lax.axis_index("expert")
    core = expert % 2
    x_here = expert // (2 * SIDE)
    z_here = (expert // 2) % SIDE
    count, width = tokens.shape
    top = expert_ids.shape[1]
    cap = count * top
    spare_cap = cap // 8
    slots = cap + spare_cap
    gate, upper, lower = w_gate[0], w_up[0], w_down[0]
    ff = gate.shape[1]
    total = jnp.sum(router_probs, axis=1, keepdims=True)
    scale = router_probs / total
    scale_b = scale.astype(BF)

    notes = jnp.concatenate(
        [
            expert_ids.T.astype(BF),
            scale_b.T,
            jnp.broadcast_to(spare_replica.reshape(N_REP, 1).astype(BF), (N_REP, count)),
        ],
        axis=0,
    )
    notes = lax.all_gather(notes, ("dp", "expert"), axis=0, tiled=False)
    notes = notes.reshape(N_REP, N_EXP, 2 * top + N_REP, count)
    ids = notes[:, :, :top].astype(jnp.int32)
    here = lax.dynamic_index_in_dim(notes, rep, 0, keepdims=False)
    scales = here[:, top : 2 * top]
    spares = here[:, 2 * top :, 0].astype(jnp.int32)

    x_all = lax.all_gather(tokens, "expert", axis=0, tiled=True)
    dy_all = lax.all_gather(cotangent, "expert", axis=0, tiled=True)

    slot, weight = placement(ids, scales, spares[expert], expert, rep, cap, spare_cap)
    sibling = expert + 1 - 2 * core
    slot_sib, _ = placement(ids, scales, spares[sibling], sibling, rep, cap, spare_cap)

    pick = one_hot(slot.reshape(-1), slots)
    row_scale = jnp.dot(pick, weight.reshape(-1, 1).astype(BF), preferred_element_type=F32)
    rows_in = jnp.dot(pick, x_all, preferred_element_type=F32).astype(BF)
    hidden = jnp.dot(rows_in, gate, preferred_element_type=F32)
    lifted = jnp.dot(rows_in, upper, preferred_element_type=F32)
    logistic = jax.nn.sigmoid(hidden)
    swished = hidden * logistic
    activated = (swished * lifted).astype(BF)
    cot_rows = jnp.dot(pick, dy_all, preferred_element_type=F32).astype(BF)
    grad_out = (row_scale * cot_rows.astype(F32)).astype(BF)

    part_lower = lax.dot_general(
        activated, grad_out, (((0,), (0,)), ((), ())), preferred_element_type=F32
    ).astype(BF)
    lower4 = part_lower.reshape(N_REP, ff // N_REP, width)

    def lower_part(d):
        return lax.dynamic_index_in_dim(lower4, (rep + d) % N_REP, 0, keepdims=False).astype(F32)

    grad_lower = ring_reduce(lower_part, along_y)

    pulled = lax.dot_general(
        cot_rows, lower, (((1,), (1,)), ((), ())), preferred_element_type=F32
    )
    shares = jnp.sum(activated.astype(F32) * pulled, axis=1).astype(BF)
    grad_act = row_scale * pulled
    grad_hidden = (grad_act * lifted * logistic * (1.0 + hidden * (1.0 - logistic))).astype(BF)
    grad_lifted = (grad_act * swished).astype(BF)

    cut = width // N_REP

    def weight_part(grad):
        def part(d):
            columns = lax.dynamic_slice_in_dim(rows_in, ((rep + d) % N_REP) * cut, cut, 1)
            return lax.dot_general(
                grad, columns, (((0,), (0,)), ((), ())), preferred_element_type=F32
            )

        return part

    back = lax.dot_general(grad_hidden, gate, (((1,), (1,)), ((), ())), preferred_element_type=F32)
    back = back + lax.dot_general(
        grad_lifted, upper, (((1,), (1,)), ((), ())), preferred_element_type=F32
    )
    back = back.astype(BF)
    grad_gate = ring_reduce(weight_part(grad_hidden), along_y)
    grad_upper = ring_reduce(weight_part(grad_lifted), along_y)

    backs = jnp.concatenate([back, other_core(back)], axis=0)
    both = jnp.stack([slot, jnp.where(slot_sib >= 0, slot_sib + slots, -1)], axis=0)
    both = both.reshape(2, SIDE, SIDE, 2, count)
    both = lax.dynamic_index_in_dim(both, core, 3, keepdims=False)
    both = jnp.roll(both, (-x_here, -z_here), axis=(1, 2))
    half = count // 2

    def spread(where):
        own, sib = where[0].reshape(-1), where[1].reshape(-1)
        iota = lax.broadcasted_iota(jnp.int32, (own.shape[0], 2 * slots), 1)
        hot = ((iota == own[:, None]) | (iota == sib[:, None])).astype(BF)
        return jnp.dot(hot, backs, preferred_element_type=F32)

    first = ring_reduce(lambda d: spread(both[:, :, d, :half]), along_z)
    second = ring_reduce(lambda d: spread(both[:, d, :, half:]), along_x)

    def last_sum(v, shift):
        v = v.reshape(SIDE, half, width)
        got = v[0]
        for d in (1, 2, 3):
            got = got + shift(v[d].astype(BF), d if d < 3 else -1).astype(F32)
        return got.astype(BF)

    token_grad = jnp.concatenate([last_sum(first, along_x), last_sum(second, along_z)], axis=0)

    share_rows = jnp.sum(
        jnp.where(
            lax.broadcasted_iota(jnp.int32, (N_EXP * count, slots), 1) == slot.reshape(-1)[:, None],
            shares.astype(F32)[None, :],
            0.0,
        ),
        axis=1,
    ).astype(BF)
    share_all = lax.all_to_all(
        share_rows.reshape(N_EXP, count), "expert", split_axis=0, concat_axis=0, tiled=True
    )
    mine = expert_ids[:, :, None] == jnp.arange(N_EXP, dtype=jnp.int32)[None, None, :]
    share = jnp.sum(jnp.where(mine, share_all.T.astype(F32)[:, None, :], 0.0), axis=2)
    prob_grad = (share - jnp.sum(scale * share, axis=1, keepdims=True)) / total

    return (
        token_grad,
        prob_grad,
        grad_gate.astype(BF).T[None],
        grad_upper.astype(BF).T[None],
        grad_lower.astype(BF)[None],
    )


def solution(mesh):
    return jax.shard_map(
        local,
        mesh=mesh,
        in_specs=(
            P(("dp", "expert"), None),
            P(("dp", "expert"), None),
            P(("dp", "expert"), None),
            P(("dp", "expert"), None),
            P("expert", None),
            P("expert", None, None),
            P("expert", None, None),
            P("expert", None, None),
        ),
        out_specs=(
            P(("dp", "expert"), None),
            P(("dp", "expert"), None),
            P("expert", "dp", None),
            P("expert", "dp", None),
            P("expert", "dp", None),
        ),
        check_vma=False,
    )
```

```python
import functools

import jax
import jax.numpy as jnp
from jax import lax
from jax.experimental import pallas as pl
from jax.experimental.pallas import tpu as pltpu
from jax.sharding import PartitionSpec as P

BF = jnp.bfloat16
F32 = jnp.float32
N_REP = 4
N_EXP = 32


def along_y(v, by):
    return lax.ppermute(v, "dp", [(r, (r + by) % N_REP) for r in range(N_REP)])


VMEM_LIMIT = 56 * 1024 * 1024


def join_wide_kernel(near_ref, far_ref, low_ref, high_ref, dep_ref, ahead_ref, behind_ref):
    half = low_ref.shape[1]
    ahead_ref[:, :half] = (near_ref[:, :half].astype(F32) + low_ref[...].astype(F32)).astype(BF)
    ahead_ref[:, half:] = near_ref[:, half:]
    behind_ref[:, :half] = far_ref[:, :half]
    behind_ref[:, half:] = (far_ref[:, half:].astype(F32) + high_ref[...].astype(F32)).astype(BF)


def join_pair_kernel(
    near_a, near_b, far_a, far_b, low_ref, high_ref, dep_ref, ahead_ref, behind_ref
):
    half = low_ref.shape[0]
    ahead_ref[:half] = (near_a[...].astype(F32) + low_ref[...].astype(F32)).astype(BF)
    ahead_ref[half:] = near_b[...]
    behind_ref[:half] = far_a[...]
    behind_ref[half:] = (far_b[...].astype(F32) + high_ref[...].astype(F32)).astype(BF)


def join(kernel, shape, arrays, dep):
    return pl.pallas_call(
        kernel,
        in_specs=[pl.BlockSpec(memory_space=pltpu.VMEM)] * len(arrays)
        + [pl.BlockSpec(memory_space=pl.ANY)],
        out_specs=[pl.BlockSpec(memory_space=pltpu.VMEM)] * 2,
        out_shape=[jax.ShapeDtypeStruct(shape, BF)] * 2,
        compiler_params=pltpu.CompilerParams(vmem_limit_bytes=VMEM_LIMIT),
        cost_estimate=pl.CostEstimate(flops=1000, bytes_accessed=1000, transcendentals=0),
    )(*arrays, dep)


def pick_kernel(most, tile, base_ref, slot_ref, rows_ref, out_ref, acc):
    group = pl.program_id(0)
    slots, width = out_ref.shape

    @pl.when(group == 0)
    def _():
        acc[...] = jnp.zeros_like(acc)

    base = pl.multiple_of(base_ref[group], 16)
    iota = lax.broadcasted_iota(jnp.int32, (most, rows_ref.shape[0]), 0) + base
    hot = (iota == slot_ref[...]).astype(BF)
    at = pl.ds(base, most)
    for w in range(0, width, tile):
        part = jnp.dot(hot, rows_ref[:, w : w + tile], preferred_element_type=F32)
        acc[at, w : w + tile] = acc[at, w : w + tile] + part.astype(BF)

    @pl.when(group == pl.num_programs(0) - 1)
    def _():
        out_ref[...] = acc[:slots, :]


def pick(rows, slot, first, slots, most_block, blocks):
    tokens, width = rows.shape
    count = tokens // first.shape[0]
    groups = first.shape[0] // blocks
    most = blocks * most_block + 16
    base = jnp.minimum(first.reshape(groups, blocks)[:, 0], slots) // 16 * 16
    return pl.pallas_call(
        functools.partial(pick_kernel, most, min(512, width)),
        grid_spec=pltpu.PrefetchScalarGridSpec(
            num_scalar_prefetch=1,
            grid=(groups,),
            in_specs=[
                pl.BlockSpec((None, 1, blocks * count), lambda g, base: (g, 0, 0)),
                pl.BlockSpec((blocks * count, width), lambda g, base: (g, 0)),
            ],
            out_specs=pl.BlockSpec((slots, width), lambda g, base: (0, 0)),
            scratch_shapes=[pltpu.VMEM((slots + most, width), BF)],
        ),
        out_shape=jax.ShapeDtypeStruct((slots, width), BF),
        compiler_params=pltpu.CompilerParams(vmem_limit_bytes=VMEM_LIMIT),
        cost_estimate=pl.CostEstimate(
            flops=2 * most * tokens * width,
            bytes_accessed=2 * width * (tokens + slots),
            transcendentals=0,
        ),
    )(base, slot.reshape(groups, 1, blocks * count), rows)


def pack_kernel(most_block, tile, first_ref, base_ref, row_ref, rows_ref, out_ref, acc):
    group = pl.program_id(0)
    slots, width = rows_ref.shape
    most = row_ref.shape[0] + 16

    @pl.when(group == 0)
    def _():
        acc[:slots, :] = rows_ref[...]
        acc[slots:, :] = jnp.zeros((acc.shape[0] - slots, width), BF)

    base = pl.multiple_of(base_ref[group], 16)
    iota = lax.broadcasted_iota(jnp.int32, (row_ref.shape[0], most), 1) + base
    hot = (iota == row_ref[...]).astype(BF)
    at = pl.ds(base, most)
    for w in range(0, width, tile):
        out_ref[:, w : w + tile] = jnp.dot(
            hot, acc[at, w : w + tile], preferred_element_type=F32
        ).astype(BF)


def pack(rows, first, most_block, blocks):
    slots, width = rows.shape
    groups = first.shape[0] // blocks
    first = jnp.minimum(first, slots)
    base = first.reshape(groups, blocks)[:, 0] // 16 * 16
    wanted = (first[:, None] + jnp.arange(most_block, dtype=jnp.int32)[None, :]).reshape(-1, 1)
    per = blocks * most_block
    return pl.pallas_call(
        functools.partial(pack_kernel, most_block, min(512, width)),
        grid_spec=pltpu.PrefetchScalarGridSpec(
            num_scalar_prefetch=2,
            grid=(groups,),
            in_specs=[
                pl.BlockSpec((per, 1), lambda g, *_: (g, 0)),
                pl.BlockSpec((slots, width), lambda g, *_: (0, 0)),
            ],
            out_specs=pl.BlockSpec((per, width), lambda g, *_: (g, 0)),
            scratch_shapes=[pltpu.VMEM((slots + per + 16, width), BF)],
        ),
        out_shape=jax.ShapeDtypeStruct((groups * per, width), BF),
        compiler_params=pltpu.CompilerParams(vmem_limit_bytes=VMEM_LIMIT),
        cost_estimate=pl.CostEstimate(
            flops=2 * groups * per * (per + 16) * width,
            bytes_accessed=2 * width * (slots + groups * per),
            transcendentals=0,
        ),
    )(first, base, wanted, rows)


def one_hot(slot, slots):
    return (lax.broadcasted_iota(jnp.int32, (slots, slot.shape[0]), 0) == slot[None, :]).astype(BF)


def placement(weight, spares, rep, cap, spare_cap):
    named = weight > 0
    load = jnp.sum(named.astype(jnp.int32))
    load = lax.all_gather(jnp.broadcast_to(load, (1, 128)), "dp", axis=0, tiled=True)[:, 0]
    excess = jnp.maximum(load - cap, 0)
    iota = jnp.arange(N_REP, dtype=jnp.int32)
    same = spares == spares[rep]
    offset = jnp.sum(jnp.where(same & (iota < rep) & (spares != iota), excess, 0))
    extra = jnp.where(spares[rep] != rep, jnp.maximum(spare_cap - offset, 0), 0)
    running, totals = running_count(named)
    before = jnp.cumsum(totals) - totals
    position = before[:, None] + running - 1
    placed = named & (position < cap + extra)
    return jnp.where(placed, position, -1), before


def running_count(named):
    count = named.shape[-1]
    upto = (
        lax.broadcasted_iota(jnp.int32, (count, count), 0)
        <= lax.broadcasted_iota(jnp.int32, (count, count), 1)
    ).astype(BF)
    running = jnp.dot(named.astype(BF), upto, preferred_element_type=F32).astype(jnp.int32)
    return running, running[:, -1]


def local(tokens, cotangent, expert_ids, router_probs, spare_replica, w_gate, w_up, w_down):
    rep = lax.axis_index("dp")
    count, width = tokens.shape
    top = expert_ids.shape[1]
    cap = count * top
    spare_cap = cap // 8
    slots = cap + spare_cap
    gate, upper, lower = w_gate[0], w_up[0], w_down[0]
    ff = gate.shape[1]
    total = jnp.sum(router_probs, axis=1, keepdims=True)
    scale = router_probs / total
    scale_b = scale.astype(BF)

    named_here = expert_ids.T[None] == jnp.arange(N_EXP, dtype=jnp.int32)[:, None, None]
    weight = jnp.sum(jnp.where(named_here, scale_b.T.astype(F32)[None], 0.0), axis=1).astype(BF)
    weight = lax.all_to_all(weight, "expert", split_axis=0, concat_axis=0, tiled=True)

    x_all = lax.all_gather(tokens, "expert", axis=0, tiled=True)
    dy_all = lax.all_gather(cotangent, "expert", axis=0, tiled=True)

    slot, first = placement(weight, spare_replica[0], rep, cap, spare_cap)

    chosen = one_hot(slot.reshape(-1), slots)
    row_scale = jnp.dot(chosen, weight.reshape(-1, 1), preferred_element_type=F32)
    most_block = min(count, 2 * count * top // N_EXP)
    rows_in = pick(x_all, slot.reshape(-1), first, slots, most_block, 4)
    hidden = jnp.dot(rows_in, gate, preferred_element_type=F32)
    lifted = jnp.dot(rows_in, upper, preferred_element_type=F32)
    logistic = jax.nn.sigmoid(hidden)
    swished = hidden * logistic
    activated = (swished * lifted).astype(BF)
    cot_rows = pick(dy_all, slot.reshape(-1), first, slots, most_block, 4)
    grad_out = (row_scale * cot_rows.astype(F32)).astype(BF)
    part_lower = lax.dot_general(
        activated, grad_out, (((0,), (0,)), ((), ())), preferred_element_type=F32
    ).astype(BF)
    rows_l, half_w = ff // N_REP, width // 2
    lower_term = [
        lax.dynamic_slice_in_dim(part_lower, ((rep + d) % N_REP) * rows_l, rows_l, 0)
        for d in range(N_REP)
    ]
    lower_low = along_y(lower_term[2][:, :half_w], 1)
    lower_high = along_y(lower_term[2][:, half_w:], -1)

    pulled = lax.dot_general(
        cot_rows, lower, (((1,), (1,)), ((), ())), preferred_element_type=F32
    )
    shares = jnp.sum(activated.astype(F32) * pulled, axis=1).astype(BF)
    grad_act = row_scale * pulled
    grad_hidden = (grad_act * lifted * logistic * (1.0 + hidden * (1.0 - logistic))).astype(BF)
    grad_lifted = (grad_act * swished).astype(BF)

    cut = width // N_REP
    columns = [
        lax.dynamic_slice_in_dim(rows_in, ((rep + d) % N_REP) * cut, cut, 1) for d in range(N_REP)
    ]

    def weight_term(grad, d):
        return lax.dot_general(
            grad, columns[d], (((0,), (0,)), ((), ())), preferred_element_type=F32
        ).astype(BF)

    gate_low = along_y(weight_term(grad_hidden, 2), 1)
    upper_high = along_y(weight_term(grad_lifted, 2), -1)

    back = lax.dot_general(grad_hidden, gate, (((1,), (1,)), ((), ())), preferred_element_type=F32)
    back = back + lax.dot_general(
        grad_lifted, upper, (((1,), (1,)), ((), ())), preferred_element_type=F32
    )
    back = back.astype(BF)
    packed = pack(back, first, most_block, 4).reshape(N_EXP, most_block, width)
    came = lax.all_to_all(packed, "expert", split_axis=0, concat_axis=0, tiled=True)

    ahead_l, behind_l = join(
        join_wide_kernel,
        (rows_l, width),
        (lower_term[1], lower_term[3], lower_low, lower_high),
        packed,
    )
    lower_got = along_y(ahead_l, 1), along_y(behind_l, -1)
    ahead, behind = join(
        join_pair_kernel,
        (2 * ff, cut),
        [weight_term(g, d) for d in (1, 3) for g in (grad_hidden, grad_lifted)]
        + [gate_low, upper_high],
        ahead_l,
    )
    weight_got = along_y(ahead, 1), along_y(behind, -1)
    named_any = jnp.any(named_here, axis=1)
    rank = jnp.where(named_any, running_count(named_any)[0] - 1, -1)
    hot = rank.T[:, :, None] == jnp.arange(most_block, dtype=jnp.int32)[None, None, :]
    token_grad = jnp.dot(
        hot.reshape(count, -1).astype(BF), came.reshape(-1, width), preferred_element_type=F32
    ).astype(BF)

    grad_lower = lower_term[0].astype(F32) + lower_got[0].astype(F32) + lower_got[1].astype(F32)
    grad_gate, grad_upper = [
        weight_term(g, 0).astype(F32) + sum(v[at : at + ff].astype(F32) for v in weight_got)
        for g, at in ((grad_hidden, 0), (grad_lifted, ff))
    ]

    share_rows = jnp.sum(
        jnp.where(
            lax.broadcasted_iota(jnp.int32, (N_EXP * count, slots), 1) == slot.reshape(-1)[:, None],
            shares.astype(F32)[None, :],
            0.0,
        ),
        axis=1,
    ).astype(BF)
    share_all = lax.all_to_all(
        share_rows.reshape(N_EXP, count), "expert", split_axis=0, concat_axis=0, tiled=True
    )
    mine = expert_ids[:, :, None] == jnp.arange(N_EXP, dtype=jnp.int32)[None, None, :]
    share = jnp.sum(jnp.where(mine, share_all.T.astype(F32)[:, None, :], 0.0), axis=2)
    prob_grad = (share - jnp.sum(scale * share, axis=1, keepdims=True)) / total

    return (
        token_grad,
        prob_grad,
        grad_gate.astype(BF).T[None],
        grad_upper.astype(BF).T[None],
        grad_lower.astype(BF)[None],
    )


def solution(mesh):
    return jax.shard_map(
        local,
        mesh=mesh,
        in_specs=(
            P(("dp", "expert"), None),
            P(("dp", "expert"), None),
            P(("dp", "expert"), None),
            P(("dp", "expert"), None),
            P("expert", None),
            P("expert", None, None),
            P("expert", None, None),
            P("expert", None, None),
        ),
        out_specs=(
            P(("dp", "expert"), None),
            P(("dp", "expert"), None),
            P("expert", "dp", None),
            P("expert", "dp", None),
            P("expert", "dp", None),
        ),
        check_vma=False,
    )
```

```python
import functools

import jax
import jax.numpy as jnp
from jax import lax
from jax.experimental import pallas as pl
from jax.experimental.pallas import tpu as pltpu
from jax.sharding import PartitionSpec as P

BF = jnp.bfloat16
F32 = jnp.float32
N_REP = 4
N_EXP = 32


LANES = 128
VMEM_LIMIT = 56 * 1024 * 1024


def pick_kernel(most, tile, base_ref, slot_ref, rows_ref, out_ref, acc):
    group = pl.program_id(0)
    slots, width = out_ref.shape

    @pl.when(group == 0)
    def _():
        acc[...] = jnp.zeros_like(acc)

    base = pl.multiple_of(base_ref[group], 16)
    iota = lax.broadcasted_iota(jnp.int32, (most, rows_ref.shape[0]), 0) + base
    hot = (iota == slot_ref[...]).astype(BF)
    at = pl.ds(base, most)
    for w in range(0, width, tile):
        part = jnp.dot(hot, rows_ref[:, w : w + tile], preferred_element_type=F32)
        acc[at, w : w + tile] = acc[at, w : w + tile] + part.astype(BF)

    @pl.when(group == pl.num_programs(0) - 1)
    def _():
        out_ref[...] = acc[:slots, :]


def pick(rows, slot, first, slots, most_block, blocks):
    tokens, width = rows.shape
    count = tokens // first.shape[0]
    groups = first.shape[0] // blocks
    most = blocks * most_block + 16
    base = jnp.minimum(first.reshape(groups, blocks)[:, 0], slots) // 16 * 16
    return pl.pallas_call(
        functools.partial(pick_kernel, most, min(512, width)),
        grid_spec=pltpu.PrefetchScalarGridSpec(
            num_scalar_prefetch=1,
            grid=(groups,),
            in_specs=[
                pl.BlockSpec((None, 1, blocks * count), lambda g, base: (g, 0, 0)),
                pl.BlockSpec((blocks * count, width), lambda g, base: (g, 0)),
            ],
            out_specs=pl.BlockSpec((slots, width), lambda g, base: (0, 0)),
            scratch_shapes=[pltpu.VMEM((slots + most, width), BF)],
        ),
        out_shape=jax.ShapeDtypeStruct((slots, width), BF),
        compiler_params=pltpu.CompilerParams(vmem_limit_bytes=VMEM_LIMIT),
        cost_estimate=pl.CostEstimate(
            flops=2 * most * tokens * width,
            bytes_accessed=2 * width * (tokens + slots),
            transcendentals=0,
        ),
    )(base, slot.reshape(groups, 1, blocks * count), rows)


def back_kernel(
    most_block, width, first_ref, hidden_ref, lifted_ref, gate_ref, upper_ref, share_ref, *refs
):
    out_ref, rows = refs[-2], refs[-1]
    slots = hidden_ref.shape[0]

    @pl.when(pl.program_id(0) == 0)
    def _():
        rows[slots:, :] = jnp.zeros((rows.shape[0] - slots, rows.shape[1]), F32)

    step = slots // 2

    @pl.loop(0, 2)
    def _(m):
        at = pl.ds(pl.multiple_of(m * step, 16), step)
        total = jnp.dot(hidden_ref[at, :], gate_ref[...], preferred_element_type=F32)
        rows[at, :] = total + jnp.dot(
            lifted_ref[at, :], upper_ref[...], preferred_element_type=F32
        )

    at_share = width % out_ref.shape[2]

    @pl.when(pl.program_id(0) == pl.num_programs(0) - 1)
    def _():
        rows[:slots, at_share:] = jnp.broadcast_to(
            share_ref[...], (slots, out_ref.shape[2] - at_share)
        )

    @pl.loop(0, out_ref.shape[0], unroll=4)
    def _(block):
        first = first_ref[block]
        base = pl.multiple_of(first // 8 * 8, 8)
        window = rows[pl.ds(base, most_block + 8), :]
        window = pltpu.roll(window, (most_block + 8 - (first - base)) % (most_block + 8), 0)
        out_ref[block] = window[:most_block].astype(BF)


def back_blocks(grad_hidden, grad_lifted, gate, upper, shares, first, most_block, deps):
    slots, ff = grad_hidden.shape
    width = gate.shape[1]
    steps = 3
    tile = (width + LANES) // steps
    blocks = first.shape[0]
    assert tile % LANES == 0 and tile * (steps - 1) < width
    return pl.pallas_call(
        functools.partial(back_kernel, most_block, width),
        grid_spec=pltpu.PrefetchScalarGridSpec(
            num_scalar_prefetch=1,
            grid=(steps,),
            in_specs=[pl.BlockSpec((slots, ff), lambda j, _: (0, 0))] * 2
            + [pl.BlockSpec((ff, tile), lambda j, _: (0, j))] * 2
            + [pl.BlockSpec((slots, 1), lambda j, _: (0, 0))]
            + [pl.BlockSpec(memory_space=pl.ANY)] * len(deps),
            out_specs=pl.BlockSpec((blocks, most_block, tile), lambda j, _: (0, 0, j)),
            scratch_shapes=[pltpu.VMEM((slots + most_block + 16, tile), F32)],
        ),
        out_shape=jax.ShapeDtypeStruct((blocks, most_block, width + LANES), BF),
        compiler_params=pltpu.CompilerParams(vmem_limit_bytes=VMEM_LIMIT),
        cost_estimate=pl.CostEstimate(
            flops=4 * slots * ff * width,
            bytes_accessed=4 * width * (ff + blocks * most_block),
            transcendentals=0,
        ),
    )(jnp.minimum(first, slots), grad_hidden, grad_lifted, gate, upper, shares[:, None], *deps)


def grads_kernel(hidden_ref, lifted_ref, rows_ref, *refs):
    out_a, out_b, left = refs[-3:]

    @pl.when(pl.program_id(0) == 0)
    def _():
        left[0] = hidden_ref[...].T
        left[1] = lifted_ref[...].T

    for n, out in enumerate((out_a, out_b)):
        out[...] = jnp.dot(left[n], rows_ref[...], preferred_element_type=F32).astype(BF)


def grads(grad_hidden, grad_lifted, rows, deps):
    slots, ff = grad_hidden.shape
    cut = rows.shape[1] // N_REP
    fixed = pl.BlockSpec((slots, ff), lambda d: (0, 0))
    return pl.pallas_call(
        grads_kernel,
        grid=(N_REP,),
        in_specs=[
            fixed,
            fixed,
            pl.BlockSpec((slots, cut), lambda d: (0, d)),
        ]
        + [pl.BlockSpec(memory_space=pl.ANY)] * len(deps),
        out_specs=[pl.BlockSpec((ff, cut), lambda d: (d, 0))] * 2,
        out_shape=[jax.ShapeDtypeStruct((N_REP * ff, cut), BF)] * 2,
        scratch_shapes=[pltpu.VMEM((2, ff, slots), BF)],
        compiler_params=pltpu.CompilerParams(vmem_limit_bytes=VMEM_LIMIT),
        cost_estimate=pl.CostEstimate(
            flops=4 * slots * ff * rows.shape[1],
            bytes_accessed=2 * rows.shape[1] * (slots + 2 * ff),
            transcendentals=0,
        ),
    )(grad_hidden, grad_lifted, rows, *deps)


def one_hot(slot, slots):
    return (lax.broadcasted_iota(jnp.int32, (slots, slot.shape[0]), 0) == slot[None, :]).astype(BF)


def placement(weight, spares, rep, cap, spare_cap):
    named = weight > 0
    load = jnp.sum(named.astype(jnp.int32))
    load = lax.all_gather(jnp.broadcast_to(load, (1, 128)), "dp", axis=0, tiled=True)[:, 0]
    excess = jnp.maximum(load - cap, 0)
    iota = jnp.arange(N_REP, dtype=jnp.int32)
    same = spares == spares[rep]
    offset = jnp.sum(jnp.where(same & (iota < rep) & (spares != iota), excess, 0))
    extra = jnp.where(spares[rep] != rep, jnp.maximum(spare_cap - offset, 0), 0)
    running, totals = running_count(named)
    before = jnp.cumsum(totals) - totals
    position = before[:, None] + running - 1
    placed = named & (position < cap + extra)
    return jnp.where(placed, position, -1), before


def running_count(named):
    count = named.shape[-1]
    upto = (
        lax.broadcasted_iota(jnp.int32, (count, count), 0)
        <= lax.broadcasted_iota(jnp.int32, (count, count), 1)
    ).astype(BF)
    running = jnp.dot(named.astype(BF), upto, preferred_element_type=F32).astype(jnp.int32)
    return running, running[:, -1]


def local(tokens, cotangent, expert_ids, router_probs, spare_replica, w_gate, w_up, w_down):
    rep = lax.axis_index("dp")
    count, width = tokens.shape
    top = expert_ids.shape[1]
    cap = count * top
    spare_cap = cap // 8
    slots = cap + spare_cap
    gate, upper, lower = w_gate[0], w_up[0], w_down[0]
    ff = gate.shape[1]
    total = jnp.sum(router_probs, axis=1, keepdims=True)
    scale = router_probs / total
    scale_b = scale.astype(BF)

    named_here = expert_ids.T[None] == jnp.arange(N_EXP, dtype=jnp.int32)[:, None, None]
    weight = jnp.sum(jnp.where(named_here, scale_b.T.astype(F32)[None], 0.0), axis=1).astype(BF)
    weight = lax.all_to_all(weight, "expert", split_axis=0, concat_axis=0, tiled=True)

    x_all = lax.all_gather(tokens, "expert", axis=0, tiled=True)
    dy_all = lax.all_gather(cotangent, "expert", axis=0, tiled=True)

    slot, first = placement(weight, spare_replica[0], rep, cap, spare_cap)

    chosen = one_hot(slot.reshape(-1), slots)
    row_scale = jnp.dot(chosen, weight.reshape(-1, 1), preferred_element_type=F32)
    most_block = min(count, 2 * count * top // N_EXP)
    rows_in = pick(x_all, slot.reshape(-1), first, slots, most_block, 4)
    hidden = jnp.dot(rows_in, gate, preferred_element_type=F32)
    lifted = jnp.dot(rows_in, upper, preferred_element_type=F32)
    logistic = jax.nn.sigmoid(hidden)
    swished = hidden * logistic
    activated = (swished * lifted).astype(BF)
    cot_rows = pick(dy_all, slot.reshape(-1), first, slots, most_block, 4)
    grad_out = (row_scale * cot_rows.astype(F32)).astype(BF)
    part_lower = lax.dot_general(
        activated, grad_out, (((0,), (0,)), ((), ())), preferred_element_type=F32
    ).astype(BF)
    grad_lower = lax.psum_scatter(part_lower, "dp", scatter_dimension=0, tiled=True)

    pulled = lax.dot_general(
        cot_rows, lower, (((1,), (1,)), ((), ())), preferred_element_type=F32
    )
    shares = jnp.sum(activated.astype(F32) * pulled, axis=1)
    grad_act = row_scale * pulled
    grad_hidden = (grad_act * lifted * logistic * (1.0 + hidden * (1.0 - logistic))).astype(BF)
    grad_lifted = (grad_act * swished).astype(BF)

    gate_parts, upper_parts = grads(grad_hidden, grad_lifted, rows_in, (part_lower,))
    grad_gate = lax.psum_scatter(gate_parts, "dp", scatter_dimension=0, tiled=True)
    grad_upper = lax.psum_scatter(upper_parts, "dp", scatter_dimension=0, tiled=True)

    packed = back_blocks(
        grad_hidden,
        grad_lifted,
        gate.T,
        upper.T,
        shares,
        first,
        most_block,
        (gate_parts, upper_parts),
    )
    came = lax.all_to_all(packed, "expert", split_axis=0, concat_axis=0, tiled=True)

    named_any = jnp.any(named_here, axis=1)
    rank = jnp.where(named_any, running_count(named_any)[0] - 1, -1).T
    hot = rank[:, :, None] == jnp.arange(most_block, dtype=jnp.int32)[None, None, :]
    token_grad = jnp.dot(
        hot.reshape(count, -1).astype(BF),
        came.reshape(-1, width + LANES),
        preferred_element_type=F32,
    )[:, :width].astype(BF)
    share_all = jnp.sum(jnp.where(hot, came[:, :, width].astype(F32)[None], 0.0), axis=2)
    mine = expert_ids[:, :, None] == jnp.arange(N_EXP, dtype=jnp.int32)[None, None, :]
    share = jnp.sum(jnp.where(mine, share_all[:, None, :], 0.0), axis=2)
    prob_grad = (share - jnp.sum(scale * share, axis=1, keepdims=True)) / total

    return (
        token_grad,
        prob_grad,
        grad_gate.T[None],
        grad_upper.T[None],
        grad_lower[None],
    )


def solution(mesh):
    return jax.shard_map(
        local,
        mesh=mesh,
        in_specs=(
            P(("dp", "expert"), None),
            P(("dp", "expert"), None),
            P(("dp", "expert"), None),
            P(("dp", "expert"), None),
            P("expert", None),
            P("expert", None, None),
            P("expert", None, None),
            P("expert", None, None),
        ),
        out_specs=(
            P(("dp", "expert"), None),
            P(("dp", "expert"), None),
            P("expert", "dp", None),
            P("expert", "dp", None),
            P("expert", "dp", None),
        ),
        check_vma=False,
    )
```

```python
import functools

import jax
import jax.numpy as jnp
from jax import lax
from jax.experimental import pallas as pl
from jax.experimental.pallas import tpu as pltpu
from jax.sharding import PartitionSpec as P

BF = jnp.bfloat16
F32 = jnp.float32
N_REP = 4
N_EXP = 32


LANES = 128


def along_y(v, by):
    return lax.ppermute(v, "dp", [(r, (r + by) % N_REP) for r in range(N_REP)])


VMEM_LIMIT = 56 * 1024 * 1024


def join_wide_kernel(near_ref, far_ref, low_ref, high_ref, dep_ref, ahead_ref, behind_ref):
    half = low_ref.shape[1]
    ahead_ref[:, :half] = (near_ref[:, :half].astype(F32) + low_ref[...].astype(F32)).astype(BF)
    ahead_ref[:, half:] = near_ref[:, half:]
    behind_ref[:, :half] = far_ref[:, :half]
    behind_ref[:, half:] = (far_ref[:, half:].astype(F32) + high_ref[...].astype(F32)).astype(BF)


def join(ahead, behind, low, high, dep):
    return pl.pallas_call(
        join_wide_kernel,
        in_specs=[pl.BlockSpec(memory_space=pltpu.VMEM)] * 4 + [pl.BlockSpec(memory_space=pl.ANY)],
        out_specs=[pl.BlockSpec(memory_space=pltpu.VMEM)] * 2,
        out_shape=[jax.ShapeDtypeStruct(ahead.shape, BF)] * 2,
        compiler_params=pltpu.CompilerParams(vmem_limit_bytes=VMEM_LIMIT),
        cost_estimate=pl.CostEstimate(flops=1000, bytes_accessed=1000, transcendentals=0),
    )(ahead, behind, low, high, dep)


def pick_kernel(most, tile, base_ref, slot_ref, rows_ref, out_ref, acc):
    group = pl.program_id(0)
    slots, width = out_ref.shape

    @pl.when(group == 0)
    def _():
        acc[...] = jnp.zeros_like(acc)

    base = pl.multiple_of(base_ref[group], 16)
    iota = lax.broadcasted_iota(jnp.int32, (most, rows_ref.shape[0]), 0) + base
    hot = (iota == slot_ref[...]).astype(BF)
    at = pl.ds(base, most)
    for w in range(0, width, tile):
        part = jnp.dot(hot, rows_ref[:, w : w + tile], preferred_element_type=F32)
        acc[at, w : w + tile] = acc[at, w : w + tile] + part.astype(BF)

    @pl.when(group == pl.num_programs(0) - 1)
    def _():
        out_ref[...] = acc[:slots, :]


def pick(rows, slot, first, slots, most_block, blocks):
    tokens, width = rows.shape
    count = tokens // first.shape[0]
    groups = first.shape[0] // blocks
    most = blocks * most_block + 16
    base = jnp.minimum(first.reshape(groups, blocks)[:, 0], slots) // 16 * 16
    return pl.pallas_call(
        functools.partial(pick_kernel, most, min(512, width)),
        grid_spec=pltpu.PrefetchScalarGridSpec(
            num_scalar_prefetch=1,
            grid=(groups,),
            in_specs=[
                pl.BlockSpec((None, 1, blocks * count), lambda g, base: (g, 0, 0)),
                pl.BlockSpec((blocks * count, width), lambda g, base: (g, 0)),
            ],
            out_specs=pl.BlockSpec((slots, width), lambda g, base: (0, 0)),
            scratch_shapes=[pltpu.VMEM((slots + most, width), BF)],
        ),
        out_shape=jax.ShapeDtypeStruct((slots, width), BF),
        compiler_params=pltpu.CompilerParams(vmem_limit_bytes=VMEM_LIMIT),
        cost_estimate=pl.CostEstimate(
            flops=2 * most * tokens * width,
            bytes_accessed=2 * width * (tokens + slots),
            transcendentals=0,
        ),
    )(base, slot.reshape(groups, 1, blocks * count), rows)


def back_kernel(
    most_block, width, first_ref, hidden_ref, lifted_ref, gate_ref, upper_ref, share_ref, *refs
):
    out_ref, rows = refs[-2], refs[-1]
    slots = hidden_ref.shape[0]

    @pl.when(pl.program_id(0) == 0)
    def _():
        rows[slots:, :] = jnp.zeros((rows.shape[0] - slots, rows.shape[1]), F32)

    step = slots // 2

    @pl.loop(0, 2)
    def _(m):
        at = pl.ds(pl.multiple_of(m * step, 16), step)
        total = jnp.dot(hidden_ref[at, :], gate_ref[...], preferred_element_type=F32)
        rows[at, :] = total + jnp.dot(
            lifted_ref[at, :], upper_ref[...], preferred_element_type=F32
        )

    at_share = width % out_ref.shape[2]

    @pl.when(pl.program_id(0) == pl.num_programs(0) - 1)
    def _():
        rows[:slots, at_share:] = jnp.broadcast_to(
            share_ref[...], (slots, out_ref.shape[2] - at_share)
        )

    @pl.loop(0, out_ref.shape[0], unroll=4)
    def _(block):
        first = first_ref[block]
        base = pl.multiple_of(first // 8 * 8, 8)
        window = rows[pl.ds(base, most_block + 8), :]
        window = pltpu.roll(window, (most_block + 8 - (first - base)) % (most_block + 8), 0)
        out_ref[block] = window[:most_block].astype(BF)


def back_blocks(grad_hidden, grad_lifted, gate, upper, shares, first, most_block, deps):
    slots, ff = grad_hidden.shape
    width = gate.shape[1]
    steps = 3
    tile = (width + LANES) // steps
    blocks = first.shape[0]
    assert tile % LANES == 0 and tile * (steps - 1) < width
    return pl.pallas_call(
        functools.partial(back_kernel, most_block, width),
        grid_spec=pltpu.PrefetchScalarGridSpec(
            num_scalar_prefetch=1,
            grid=(steps,),
            in_specs=[pl.BlockSpec((slots, ff), lambda j, _: (0, 0))] * 2
            + [pl.BlockSpec((ff, tile), lambda j, _: (0, j))] * 2
            + [pl.BlockSpec((slots, 1), lambda j, _: (0, 0))]
            + [pl.BlockSpec(memory_space=pl.ANY)] * len(deps),
            out_specs=pl.BlockSpec((blocks, most_block, tile), lambda j, _: (0, 0, j)),
            scratch_shapes=[pltpu.VMEM((slots + most_block + 16, tile), F32)],
        ),
        out_shape=jax.ShapeDtypeStruct((blocks, most_block, width + LANES), BF),
        compiler_params=pltpu.CompilerParams(vmem_limit_bytes=VMEM_LIMIT),
        cost_estimate=pl.CostEstimate(
            flops=4 * slots * ff * width,
            bytes_accessed=4 * width * (ff + blocks * most_block),
            transcendentals=0,
        ),
    )(jnp.minimum(first, slots), grad_hidden, grad_lifted, gate, upper, shares[:, None], *deps)


def grads_kernel(hidden_ref, lifted_ref, rows_ref, *refs):
    out_a, out_b, left = refs[-3:]

    @pl.when(pl.program_id(0) == 0)
    def _():
        left[0] = hidden_ref[...].T
        left[1] = lifted_ref[...].T

    for n, out in enumerate((out_a, out_b)):
        out[...] = jnp.dot(left[n], rows_ref[...], preferred_element_type=F32).astype(BF)


def grads(grad_hidden, grad_lifted, rows, deps):
    slots, ff = grad_hidden.shape
    cut = rows.shape[1] // N_REP
    fixed = pl.BlockSpec((slots, ff), lambda d: (0, 0))
    return pl.pallas_call(
        grads_kernel,
        grid=(N_REP,),
        in_specs=[
            fixed,
            fixed,
            pl.BlockSpec((slots, cut), lambda d: (0, d)),
        ]
        + [pl.BlockSpec(memory_space=pl.ANY)] * len(deps),
        out_specs=[pl.BlockSpec((ff, cut), lambda d: (d, 0))] * 2,
        out_shape=[jax.ShapeDtypeStruct((N_REP * ff, cut), BF)] * 2,
        scratch_shapes=[pltpu.VMEM((2, ff, slots), BF)],
        compiler_params=pltpu.CompilerParams(vmem_limit_bytes=VMEM_LIMIT),
        cost_estimate=pl.CostEstimate(
            flops=4 * slots * ff * rows.shape[1],
            bytes_accessed=2 * rows.shape[1] * (slots + 2 * ff),
            transcendentals=0,
        ),
    )(grad_hidden, grad_lifted, rows, *deps)


def one_hot(slot, slots):
    return (lax.broadcasted_iota(jnp.int32, (slots, slot.shape[0]), 0) == slot[None, :]).astype(BF)


def placement(weight, spares, rep, cap, spare_cap):
    named = weight > 0
    load = jnp.sum(named.astype(jnp.int32))
    load = lax.all_gather(jnp.broadcast_to(load, (1, 128)), "dp", axis=0, tiled=True)[:, 0]
    excess = jnp.maximum(load - cap, 0)
    iota = jnp.arange(N_REP, dtype=jnp.int32)
    same = spares == spares[rep]
    offset = jnp.sum(jnp.where(same & (iota < rep) & (spares != iota), excess, 0))
    extra = jnp.where(spares[rep] != rep, jnp.maximum(spare_cap - offset, 0), 0)
    running, totals = running_count(named)
    before = jnp.cumsum(totals) - totals
    position = before[:, None] + running - 1
    placed = named & (position < cap + extra)
    return jnp.where(placed, position, -1), before


def running_count(named):
    count = named.shape[-1]
    upto = (
        lax.broadcasted_iota(jnp.int32, (count, count), 0)
        <= lax.broadcasted_iota(jnp.int32, (count, count), 1)
    ).astype(BF)
    running = jnp.dot(named.astype(BF), upto, preferred_element_type=F32).astype(jnp.int32)
    return running, running[:, -1]


def local(tokens, cotangent, expert_ids, router_probs, spare_replica, w_gate, w_up, w_down):
    rep = lax.axis_index("dp")
    count, width = tokens.shape
    top = expert_ids.shape[1]
    cap = count * top
    spare_cap = cap // 8
    slots = cap + spare_cap
    gate, upper, lower = w_gate[0], w_up[0], w_down[0]
    ff = gate.shape[1]
    total = jnp.sum(router_probs, axis=1, keepdims=True)
    scale = router_probs / total
    scale_b = scale.astype(BF)

    named_here = expert_ids.T[None] == jnp.arange(N_EXP, dtype=jnp.int32)[:, None, None]
    weight = jnp.sum(jnp.where(named_here, scale_b.T.astype(F32)[None], 0.0), axis=1).astype(BF)
    weight = lax.all_to_all(weight, "expert", split_axis=0, concat_axis=0, tiled=True)

    x_all = lax.all_gather(tokens, "expert", axis=0, tiled=True)
    dy_all = lax.all_gather(cotangent, "expert", axis=0, tiled=True)

    slot, first = placement(weight, spare_replica[0], rep, cap, spare_cap)

    chosen = one_hot(slot.reshape(-1), slots)
    row_scale = jnp.dot(chosen, weight.reshape(-1, 1), preferred_element_type=F32)
    most_block = min(count, 2 * count * top // N_EXP)
    rows_in = pick(x_all, slot.reshape(-1), first, slots, most_block, 4)
    hidden = jnp.dot(rows_in, gate, preferred_element_type=F32)
    lifted = jnp.dot(rows_in, upper, preferred_element_type=F32)
    logistic = jax.nn.sigmoid(hidden)
    swished = hidden * logistic
    activated = (swished * lifted).astype(BF)
    cot_rows = pick(dy_all, slot.reshape(-1), first, slots, most_block, 4)
    grad_out = (row_scale * cot_rows.astype(F32)).astype(BF)
    part_lower = lax.dot_general(
        activated, grad_out, (((0,), (0,)), ((), ())), preferred_element_type=F32
    ).astype(BF)
    rows_l, half_w = ff // N_REP, width // 2
    lower_term = [
        lax.dynamic_slice_in_dim(part_lower, ((rep + d) % N_REP) * rows_l, rows_l, 0)
        for d in range(N_REP)
    ]
    lower_low = along_y(lower_term[2][:, :half_w], 1)
    lower_high = along_y(lower_term[2][:, half_w:], -1)

    pulled = lax.dot_general(
        cot_rows, lower, (((1,), (1,)), ((), ())), preferred_element_type=F32
    )
    shares = jnp.sum(activated.astype(F32) * pulled, axis=1)
    grad_act = row_scale * pulled
    grad_hidden = (grad_act * lifted * logistic * (1.0 + hidden * (1.0 - logistic))).astype(BF)
    grad_lifted = (grad_act * swished).astype(BF)

    gate_parts, upper_parts = grads(grad_hidden, grad_lifted, rows_in, ())
    grad_gate = lax.psum_scatter(gate_parts, "dp", scatter_dimension=0, tiled=True)
    grad_upper = lax.psum_scatter(upper_parts, "dp", scatter_dimension=0, tiled=True)

    packed = back_blocks(
        grad_hidden,
        grad_lifted,
        gate.T,
        upper.T,
        shares,
        first,
        most_block,
        (gate_parts, upper_parts),
    )
    came = lax.all_to_all(packed, "expert", split_axis=0, concat_axis=0, tiled=True)
    ahead, behind = join(lower_term[1], lower_term[3], lower_low, lower_high, packed)
    lower_got = along_y(ahead, 1), along_y(behind, -1)
    grad_lower = (
        lower_term[0].astype(F32) + lower_got[0].astype(F32) + lower_got[1].astype(F32)
    ).astype(BF)

    named_any = jnp.any(named_here, axis=1)
    rank = jnp.where(named_any, running_count(named_any)[0] - 1, -1).T
    hot = rank[:, :, None] == jnp.arange(most_block, dtype=jnp.int32)[None, None, :]
    token_grad = jnp.dot(
        hot.reshape(count, -1).astype(BF),
        came.reshape(-1, width + LANES),
        preferred_element_type=F32,
    )[:, :width].astype(BF)
    share_all = jnp.sum(jnp.where(hot, came[:, :, width].astype(F32)[None], 0.0), axis=2)
    mine = expert_ids[:, :, None] == jnp.arange(N_EXP, dtype=jnp.int32)[None, None, :]
    share = jnp.sum(jnp.where(mine, share_all[:, None, :], 0.0), axis=2)
    prob_grad = (share - jnp.sum(scale * share, axis=1, keepdims=True)) / total

    return (
        token_grad,
        prob_grad,
        grad_gate.T[None],
        grad_upper.T[None],
        grad_lower[None],
    )


def solution(mesh):
    return jax.shard_map(
        local,
        mesh=mesh,
        in_specs=(
            P(("dp", "expert"), None),
            P(("dp", "expert"), None),
            P(("dp", "expert"), None),
            P(("dp", "expert"), None),
            P("expert", None),
            P("expert", None, None),
            P("expert", None, None),
            P("expert", None, None),
        ),
        out_specs=(
            P(("dp", "expert"), None),
            P(("dp", "expert"), None),
            P("expert", "dp", None),
            P("expert", "dp", None),
            P("expert", "dp", None),
        ),
        check_vma=False,
    )
```

```python
import functools

import jax
import jax.numpy as jnp
from jax import lax
from jax.experimental import pallas as pl
from jax.experimental.pallas import tpu as pltpu
from jax.sharding import PartitionSpec as P

BF = jnp.bfloat16
F32 = jnp.float32
N_REP = 4
N_EXP = 32


LANES = 128


def along_y(v, by):
    return lax.ppermute(v, "dp", [(r, (r + by) % N_REP) for r in range(N_REP)])


VMEM_LIMIT = 56 * 1024 * 1024


def join_wide_kernel(near_ref, far_ref, low_ref, high_ref, dep_ref, ahead_ref, behind_ref):
    half = low_ref.shape[1]
    ahead_ref[:, :half] = (near_ref[:, :half].astype(F32) + low_ref[...].astype(F32)).astype(BF)
    ahead_ref[:, half:] = near_ref[:, half:]
    behind_ref[:, :half] = far_ref[:, :half]
    behind_ref[:, half:] = (far_ref[:, half:].astype(F32) + high_ref[...].astype(F32)).astype(BF)


def join(ahead, behind, low, high, dep):
    return pl.pallas_call(
        join_wide_kernel,
        in_specs=[pl.BlockSpec(memory_space=pltpu.VMEM)] * 4 + [pl.BlockSpec(memory_space=pl.ANY)],
        out_specs=[pl.BlockSpec(memory_space=pltpu.VMEM)] * 2,
        out_shape=[jax.ShapeDtypeStruct(ahead.shape, BF)] * 2,
        compiler_params=pltpu.CompilerParams(vmem_limit_bytes=VMEM_LIMIT),
        cost_estimate=pl.CostEstimate(flops=1000, bytes_accessed=1000, transcendentals=0),
    )(ahead, behind, low, high, dep)


def pick_kernel(most, tile, base_ref, slot_ref, rows_ref, out_ref, acc):
    group = pl.program_id(0)
    slots, width = out_ref.shape

    @pl.when(group == 0)
    def _():
        acc[...] = jnp.zeros_like(acc)

    base = pl.multiple_of(base_ref[group], 16)
    iota = lax.broadcasted_iota(jnp.int32, (most, rows_ref.shape[0]), 0) + base
    hot = (iota == slot_ref[...]).astype(BF)
    at = pl.ds(base, most)
    for w in range(0, width, tile):
        part = jnp.dot(hot, rows_ref[:, w : w + tile], preferred_element_type=F32)
        acc[at, w : w + tile] = acc[at, w : w + tile] + part.astype(BF)

    @pl.when(group == pl.num_programs(0) - 1)
    def _():
        out_ref[...] = acc[:slots, :]


def pick(rows, slot, first, slots, most_block, blocks):
    tokens, width = rows.shape
    count = tokens // first.shape[0]
    groups = first.shape[0] // blocks
    most = blocks * most_block + 16
    base = jnp.minimum(first.reshape(groups, blocks)[:, 0], slots) // 16 * 16
    return pl.pallas_call(
        functools.partial(pick_kernel, most, min(512, width)),
        grid_spec=pltpu.PrefetchScalarGridSpec(
            num_scalar_prefetch=1,
            grid=(groups,),
            in_specs=[
                pl.BlockSpec((None, 1, blocks * count), lambda g, base: (g, 0, 0)),
                pl.BlockSpec((blocks * count, width), lambda g, base: (g, 0)),
            ],
            out_specs=pl.BlockSpec((slots, width), lambda g, base: (0, 0)),
            scratch_shapes=[pltpu.VMEM((slots + most, width), BF)],
        ),
        out_shape=jax.ShapeDtypeStruct((slots, width), BF),
        compiler_params=pltpu.CompilerParams(vmem_limit_bytes=VMEM_LIMIT),
        cost_estimate=pl.CostEstimate(
            flops=2 * most * tokens * width,
            bytes_accessed=2 * width * (tokens + slots),
            transcendentals=0,
        ),
    )(base, slot.reshape(groups, 1, blocks * count), rows)


def inner_kernel(cot_ref, lower_ref, hidden_ref, lifted_ref, act_ref, scale_ref, out_h, out_l, share):
    pulled = lax.dot_general(
        cot_ref[...], lower_ref[...], (((1,), (1,)), ((), ())), preferred_element_type=F32
    )
    hidden = hidden_ref[...]
    logistic = jax.nn.sigmoid(hidden)
    share[...] = jnp.sum(act_ref[...].astype(F32) * pulled, axis=1, keepdims=True)
    grad_act = scale_ref[...] * pulled
    out_h[...] = (
        grad_act * lifted_ref[...] * logistic * (1.0 + hidden * (1.0 - logistic))
    ).astype(BF)
    out_l[...] = (grad_act * (hidden * logistic)).astype(BF)


def inner_grads(cot_rows, lower, hidden, lifted, activated, row_scale):
    slots, ff = hidden.shape
    step = slots // 3
    wide = pl.BlockSpec((step, ff), lambda m: (m, 0))
    one = pl.BlockSpec((step, 1), lambda m: (m, 0))
    return pl.pallas_call(
        inner_kernel,
        grid=(3,),
        in_specs=[
            pl.BlockSpec((step, lower.shape[1]), lambda m: (m, 0)),
            pl.BlockSpec(lower.shape, lambda m: (0, 0)),
            wide,
            wide,
            wide,
            one,
        ],
        out_specs=[wide, wide, one],
        out_shape=[jax.ShapeDtypeStruct((slots, ff), BF)] * 2
        + [jax.ShapeDtypeStruct((slots, 1), F32)],
        compiler_params=pltpu.CompilerParams(vmem_limit_bytes=VMEM_LIMIT),
    )(cot_rows, lower, hidden, lifted, activated, row_scale)


def back_kernel(
    most_block, width, first_ref, hidden_ref, lifted_ref, gate_ref, upper_ref, share_ref, *refs
):
    out_ref, rows = refs[-2], refs[-1]
    slots = hidden_ref.shape[0]

    @pl.when(pl.program_id(0) == 0)
    def _():
        rows[slots:, :] = jnp.zeros((rows.shape[0] - slots, rows.shape[1]), F32)

    step = slots // 2

    @pl.loop(0, 2)
    def _(m):
        at = pl.ds(pl.multiple_of(m * step, 16), step)
        total = jnp.dot(hidden_ref[at, :], gate_ref[...], preferred_element_type=F32)
        rows[at, :] = total + jnp.dot(
            lifted_ref[at, :], upper_ref[...], preferred_element_type=F32
        )

    at_share = width % out_ref.shape[2]

    @pl.when(pl.program_id(0) == pl.num_programs(0) - 1)
    def _():
        rows[:slots, at_share:] = jnp.broadcast_to(
            share_ref[...], (slots, out_ref.shape[2] - at_share)
        )

    @pl.loop(0, out_ref.shape[0], unroll=4)
    def _(block):
        first = first_ref[block]
        base = pl.multiple_of(first // 8 * 8, 8)
        window = rows[pl.ds(base, most_block + 8), :]
        window = pltpu.roll(window, (most_block + 8 - (first - base)) % (most_block + 8), 0)
        out_ref[block] = window[:most_block].astype(BF)


def back_blocks(grad_hidden, grad_lifted, gate, upper, shares, first, most_block, deps):
    slots, ff = grad_hidden.shape
    width = gate.shape[1]
    steps = 3
    tile = (width + LANES) // steps
    blocks = first.shape[0]
    assert tile % LANES == 0 and tile * (steps - 1) < width
    return pl.pallas_call(
        functools.partial(back_kernel, most_block, width),
        grid_spec=pltpu.PrefetchScalarGridSpec(
            num_scalar_prefetch=1,
            grid=(steps,),
            in_specs=[pl.BlockSpec((slots, ff), lambda j, _: (0, 0))] * 2
            + [pl.BlockSpec((ff, tile), lambda j, _: (0, j))] * 2
            + [pl.BlockSpec((slots, 1), lambda j, _: (0, 0))]
            + [pl.BlockSpec(memory_space=pl.ANY)] * len(deps),
            out_specs=pl.BlockSpec((blocks, most_block, tile), lambda j, _: (0, 0, j)),
            scratch_shapes=[pltpu.VMEM((slots + most_block + 16, tile), F32)],
        ),
        out_shape=jax.ShapeDtypeStruct((blocks, most_block, width + LANES), BF),
        compiler_params=pltpu.CompilerParams(vmem_limit_bytes=VMEM_LIMIT),
        cost_estimate=pl.CostEstimate(
            flops=4 * slots * ff * width,
            bytes_accessed=4 * width * (ff + blocks * most_block),
            transcendentals=0,
        ),
    )(jnp.minimum(first, slots), grad_hidden, grad_lifted, gate, upper, shares[:, None], *deps)


def grads_kernel(hidden_ref, lifted_ref, rows_ref, *refs):
    out_a, out_b, left = refs[-3:]

    @pl.when(pl.program_id(0) == 0)
    def _():
        left[0] = hidden_ref[...].T
        left[1] = lifted_ref[...].T

    for n, out in enumerate((out_a, out_b)):
        out[...] = jnp.dot(left[n], rows_ref[...], preferred_element_type=F32).astype(BF)


def grads(grad_hidden, grad_lifted, rows, deps):
    slots, ff = grad_hidden.shape
    cut = rows.shape[1] // N_REP
    fixed = pl.BlockSpec((slots, ff), lambda d: (0, 0))
    return pl.pallas_call(
        grads_kernel,
        grid=(N_REP,),
        in_specs=[
            fixed,
            fixed,
            pl.BlockSpec((slots, cut), lambda d: (0, d)),
        ]
        + [pl.BlockSpec(memory_space=pl.ANY)] * len(deps),
        out_specs=[pl.BlockSpec((ff, cut), lambda d: (d, 0))] * 2,
        out_shape=[jax.ShapeDtypeStruct((N_REP * ff, cut), BF)] * 2,
        scratch_shapes=[pltpu.VMEM((2, ff, slots), BF)],
        compiler_params=pltpu.CompilerParams(vmem_limit_bytes=VMEM_LIMIT),
        cost_estimate=pl.CostEstimate(
            flops=4 * slots * ff * rows.shape[1],
            bytes_accessed=2 * rows.shape[1] * (slots + 2 * ff),
            transcendentals=0,
        ),
    )(grad_hidden, grad_lifted, rows, *deps)


def one_hot(slot, slots):
    return (lax.broadcasted_iota(jnp.int32, (slots, slot.shape[0]), 0) == slot[None, :]).astype(BF)


def placement(weight, spares, rep, cap, spare_cap):
    named = weight > 0
    load = jnp.sum(named.astype(jnp.int32))
    load = lax.all_gather(jnp.broadcast_to(load, (1, 128)), "dp", axis=0, tiled=True)[:, 0]
    excess = jnp.maximum(load - cap, 0)
    iota = jnp.arange(N_REP, dtype=jnp.int32)
    same = spares == spares[rep]
    offset = jnp.sum(jnp.where(same & (iota < rep) & (spares != iota), excess, 0))
    extra = jnp.where(spares[rep] != rep, jnp.maximum(spare_cap - offset, 0), 0)
    running, totals = running_count(named)
    before = jnp.cumsum(totals) - totals
    position = before[:, None] + running - 1
    placed = named & (position < cap + extra)
    return jnp.where(placed, position, -1), before


def running_count(named):
    count = named.shape[-1]
    upto = (
        lax.broadcasted_iota(jnp.int32, (count, count), 0)
        <= lax.broadcasted_iota(jnp.int32, (count, count), 1)
    ).astype(BF)
    running = jnp.dot(named.astype(BF), upto, preferred_element_type=F32).astype(jnp.int32)
    return running, running[:, -1]


def local(tokens, cotangent, expert_ids, router_probs, spare_replica, w_gate, w_up, w_down):
    rep = lax.axis_index("dp")
    count, width = tokens.shape
    top = expert_ids.shape[1]
    cap = count * top
    spare_cap = cap // 8
    slots = cap + spare_cap
    gate, upper, lower = w_gate[0], w_up[0], w_down[0]
    ff = gate.shape[1]
    total = jnp.sum(router_probs, axis=1, keepdims=True)
    scale = router_probs / total
    scale_b = scale.astype(BF)

    named_here = expert_ids.T[None] == jnp.arange(N_EXP, dtype=jnp.int32)[:, None, None]
    weight = jnp.sum(jnp.where(named_here, scale_b.T.astype(F32)[None], 0.0), axis=1).astype(BF)
    weight = lax.all_to_all(weight, "expert", split_axis=0, concat_axis=0, tiled=True)

    x_all = lax.all_gather(tokens, "expert", axis=0, tiled=True)
    dy_all = lax.all_gather(cotangent, "expert", axis=0, tiled=True)

    slot, first = placement(weight, spare_replica[0], rep, cap, spare_cap)

    chosen = one_hot(slot.reshape(-1), slots)
    row_scale = jnp.dot(chosen, weight.reshape(-1, 1), preferred_element_type=F32)
    most_block = min(count, 2 * count * top // N_EXP)
    rows_in = pick(x_all, slot.reshape(-1), first, slots, most_block, 4)
    hidden = jnp.dot(rows_in, gate, preferred_element_type=F32)
    lifted = jnp.dot(rows_in, upper, preferred_element_type=F32)
    logistic = jax.nn.sigmoid(hidden)
    swished = hidden * logistic
    activated = (swished * lifted).astype(BF)
    cot_rows = pick(dy_all, slot.reshape(-1), first, slots, most_block, 4)
    grad_out = (row_scale * cot_rows.astype(F32)).astype(BF)
    part_lower = lax.dot_general(
        activated, grad_out, (((0,), (0,)), ((), ())), preferred_element_type=F32
    ).astype(BF)
    rows_l, half_w = ff // N_REP, width // 2
    lower_term = [
        lax.dynamic_slice_in_dim(part_lower, ((rep + d) % N_REP) * rows_l, rows_l, 0)
        for d in range(N_REP)
    ]
    lower_low = along_y(lower_term[2][:, :half_w], 1)
    lower_high = along_y(lower_term[2][:, half_w:], -1)

    grad_hidden, grad_lifted, shares = inner_grads(
        cot_rows, lower, hidden, lifted, activated, row_scale
    )
    shares = shares[:, 0]

    gate_parts, upper_parts = grads(grad_hidden, grad_lifted, rows_in, ())
    grad_gate = lax.psum_scatter(gate_parts, "dp", scatter_dimension=0, tiled=True)
    grad_upper = lax.psum_scatter(upper_parts, "dp", scatter_dimension=0, tiled=True)

    packed = back_blocks(
        grad_hidden,
        grad_lifted,
        gate.T,
        upper.T,
        shares,
        first,
        most_block,
        (gate_parts, upper_parts),
    )
    came = lax.all_to_all(packed, "expert", split_axis=0, concat_axis=0, tiled=True)
    ahead, behind = join(lower_term[1], lower_term[3], lower_low, lower_high, packed)
    lower_got = along_y(ahead, 1), along_y(behind, -1)
    grad_lower = (
        lower_term[0].astype(F32) + lower_got[0].astype(F32) + lower_got[1].astype(F32)
    ).astype(BF)

    named_any = jnp.any(named_here, axis=1)
    rank = jnp.where(named_any, running_count(named_any)[0] - 1, -1).T
    hot = rank[:, :, None] == jnp.arange(most_block, dtype=jnp.int32)[None, None, :]
    token_grad = jnp.dot(
        hot.reshape(count, -1).astype(BF),
        came.reshape(-1, width + LANES),
        preferred_element_type=F32,
    )[:, :width].astype(BF)
    share_all = jnp.sum(jnp.where(hot, came[:, :, width].astype(F32)[None], 0.0), axis=2)
    mine = expert_ids[:, :, None] == jnp.arange(N_EXP, dtype=jnp.int32)[None, None, :]
    share = jnp.sum(jnp.where(mine, share_all[:, None, :], 0.0), axis=2)
    prob_grad = (share - jnp.sum(scale * share, axis=1, keepdims=True)) / total

    return (
        token_grad,
        prob_grad,
        grad_gate.T[None],
        grad_upper.T[None],
        grad_lower[None],
    )


def solution(mesh):
    return jax.shard_map(
        local,
        mesh=mesh,
        in_specs=(
            P(("dp", "expert"), None),
            P(("dp", "expert"), None),
            P(("dp", "expert"), None),
            P(("dp", "expert"), None),
            P("expert", None),
            P("expert", None, None),
            P("expert", None, None),
            P("expert", None, None),
        ),
        out_specs=(
            P(("dp", "expert"), None),
            P(("dp", "expert"), None),
            P("expert", "dp", None),
            P("expert", "dp", None),
            P("expert", "dp", None),
        ),
        check_vma=False,
    )
```
